512 devices in a mesh: dp: 32 (over z_hi, y), tensor: 16 (over x, z_lo, core).
Axes of the slice: x: 4, y: 8, z: 8 (z_hi: 4, z_lo: 2; z = z_hi * 2 + z_lo), core: 2. Of those that a mesh axis runs over, the one named last changes fastest.
Arguments:
- hidden: bfloat16 [6144, 14336], P('dp', 'tensor'), may hold values from -6 to 6
- down_rotated: bfloat16 [14336, 4096], P('tensor', 'dp'), may hold values from -0.09375 to 0.09375
- out_gradient: bfloat16 [6144, 4096], P('dp', 'tensor'), may hold values from -6 to 6
- sign_bits: int32 [14336], P('tensor'), may hold values from 0 to 1
- act_exponent: int32 [6144], P('dp'), may hold values from -7 to -3
- grad_exponent: int32 [6144], P('dp'), may hold values from -7 to -3
Outputs:
- mixed: bfloat16 [6144, 4096], P('dp', 'tensor')
- grad_hidden: bfloat16 [6144, 14336], P('dp', 'tensor')
The draws below stay inside these ranges and needn't reach their ends.
Inputs may be any that keep to these rules, and one draw needn't show every extreme that they name: `sign_bits`: 0 means the sign +1, 1 means -1.
All inputs are finite; a program needn't handle non-finite values.
Results may differ from the reference program's by a relative error of at most 0.028.
Values may be sent and summed in bfloat16 or wider, within the bound.
No kernel may reach another device: no remote copies, remote signals or barrier semaphores. Data moves between devices by JAX's collectives and lax.ppermute only.
A program may use at most 64 MiB of HBM per device.

```python
import jax
import jax.numpy as jnp
from jax import lax

D = 4096
FF = 14336
BLK = 128
TOKENS = 6144
N_TENSOR = 16


def with_ends(drawn, key, least, largest):
    extent = drawn.shape
    index_at = [jax.random.randint(jax.random.fold_in(key, axis), (), 0, extent[axis]) for axis in range(len(extent))]
    drawn = drawn.at[tuple(index_at)].set(least)
    longest = extent.index(max(extent))
    index_at[longest] = (index_at[longest] + 1) % extent[longest]
    return drawn.at[tuple(index_at)].set(largest)


def strengthened(result, own_key, source, target, parts, factor):
    def block_of(dim):
        return (jnp.arange(result.shape[dim]) // (result.shape[dim] // parts)).reshape((-1,) + (1,) * (result.ndim - 1 - dim))

    one_side = jax.random.permutation(own_key, parts)[block_of(target)]
    second = (block_of(target) + parts // 2) % parts
    return jnp.where((block_of(source) == one_side) | (block_of(source) == second), factor * result, result)


def shard_levels(stream_key, dims, pieces, smallest, high):
    factor_of = 1.0
    for axis_at, shards_of in pieces:
        steps = jax.random.uniform(jax.random.fold_in(jax.random.fold_in(stream_key, 6), axis_at), (shards_of,), jnp.float32, smallest / len(pieces), high / len(pieces))
        factor_of = factor_of * jnp.repeat(jnp.exp(steps), dims[axis_at] // shards_of).reshape((-1,) + (1,) * (len(dims) - 1 - axis_at))
    return factor_of


def centred(stream_key, dims, spread, limit, pieces=(), kind=jnp.bfloat16):
    entries = spread * jax.random.normal(stream_key, dims, jnp.float32)
    if pieces:
        entries = entries * shard_levels(stream_key, dims, pieces, -0.22, 0.18)
    return jnp.clip(entries, -limit, limit).astype(kind)


def noise_with(stream_key, dims, deviation, reach, cuts, heavy, kind=jnp.bfloat16):
    values = deviation * jax.random.normal(stream_key, dims, jnp.float32)
    if cuts:
        values = values * shard_levels(stream_key, dims, cuts, -0.22, 0.18)
    return jnp.clip(strengthened(values, jax.random.fold_in(stream_key, 3), *heavy), -reach, reach).astype(kind)


def setup_inputs(seed: int = 0) -> dict:
    arg_keys = jax.random.split(jax.random.key(seed), 7)
    return {
        "hidden": centred(arg_keys[0], (TOKENS, FF), 1.0, 6.0, ((0, 32), (1, 16))),
        "down_rotated": noise_with(arg_keys[1], (FF, D), FF ** -0.5, 0.09375, ((0, 16), (1, 32)), (0, 1, 32, 2.75)),
        "out_gradient": centred(arg_keys[2], (TOKENS, D), 1.0, 6.0, ((0, 32), (1, 16))),
        "sign_bits": with_ends(jax.random.randint(arg_keys[3], (FF,), 0, 2), jax.random.fold_in(arg_keys[3], 1), 0, 1).astype(jnp.int32),
        "act_exponent": with_ends(jax.random.randint(arg_keys[4], (TOKENS,), -7, -2), jax.random.fold_in(arg_keys[4], 1), -7, (-2) - 1).astype(jnp.int32),
        "grad_exponent": with_ends(jax.random.randint(arg_keys[5], (TOKENS,), -7, -2), jax.random.fold_in(arg_keys[5], 1), -7, (-2) - 1).astype(jnp.int32),
    }


def hadamard(order):
    index = jnp.arange(order, dtype=jnp.int32)
    intersection_bits = index[:, None] & index[None, :]
    parity = jnp.zeros((order, order), jnp.int32)
    for bit_number in range(order.bit_length() - 1):
        parity = parity ^ ((intersection_bits >> bit_number) & 1)
    return (1 - 2 * parity).astype(jnp.float32)


def both_factors(values):
    count = values.shape[0]
    local_table = hadamard(BLK)
    cross_table = hadamard(N_TENSOR)
    shaped = values.reshape(count, N_TENSOR, FF // (N_TENSOR * BLK), BLK)
    shaped = jnp.einsum("rnbk,kj->rnbj", shaped, local_table, precision=lax.Precision.HIGHEST)
    shaped = jnp.einsum("rnbj,mn->rmbj", shaped, cross_table, precision=lax.Precision.HIGHEST)
    factor = 1.0 / (float(N_TENSOR * BLK) ** 0.5)
    return shaped.reshape(count, FF) * factor


def reference(hidden, down_rotated, out_gradient, sign_bits, act_exponent, grad_exponent):
    flips = (1 - 2 * sign_bits).astype(jnp.float32)
    rotated = both_factors(hidden.astype(jnp.float32) * flips[None, :])
    act_factor = jnp.exp2(act_exponent.astype(jnp.float32))[:, None]
    act_grid = jnp.clip(rotated / act_factor, -127.0, 127.0).astype(jnp.bfloat16)
    width = FF // N_TENSOR

    def add_part(shard, running):
        start = (shard * width).astype(jnp.int32)
        columns = lax.dynamic_slice_in_dim(act_grid, start, width, 1)
        rows = lax.dynamic_slice_in_dim(down_rotated, start, width, 0)
        part = jnp.dot(columns, rows, preferred_element_type=jnp.float32)
        return running + lax.optimization_barrier(part.astype(jnp.bfloat16)).astype(jnp.float32)

    summed = lax.fori_loop(0, N_TENSOR, add_part, jnp.zeros((TOKENS, D), jnp.float32))
    mixed = (summed * act_factor).astype(jnp.bfloat16)
    grad_factor = jnp.exp2(grad_exponent.astype(jnp.float32))[:, None]
    grad_grid = jnp.clip(out_gradient.astype(jnp.float32) / grad_factor, -127.0, 127.0).astype(jnp.bfloat16)
    grad_rot = jnp.dot(grad_grid, down_rotated.T, preferred_element_type=jnp.float32) * grad_factor
    grad_hidden = (both_factors(grad_rot) * flips[None, :]).astype(jnp.bfloat16)
    return mixed, grad_hidden
```

```python
import functools

import jax
import jax.numpy as jnp
import numpy as np
from jax import lax
from jax.experimental import pallas as pl
from jax.experimental.pallas import tpu as pltpu
from jax.sharding import Mesh, PartitionSpec as P

BLK = 128
TENSOR = ("x", "zl", "core")
DP = ("zh", "y")
BF = jnp.bfloat16
F32 = jnp.float32
SC_ROWS = 448


def sylvester(order):
    index = np.arange(order)
    bits = index[:, None] & index[None, :]
    parity = np.zeros((order, order), np.int64)
    for bit in range(order.bit_length() - 1):
        parity ^= (bits >> bit) & 1
    return 1.0 - 2.0 * parity


def shifted(value, axis, step):
    size = lax.axis_size(axis)
    return lax.ppermute(value, axis, [(i, (i + step) % size) for i in range(size)])


def exchange(value):
    return lax.all_to_all(value, TENSOR, 0, 0)


def hadamard_kernel(limit, table_ref, x_ref, out_ref, mixed_ref):
    parts, rows, _ = x_ref.shape
    for n in range(parts):
        mixed_ref[n] = jnp.dot(x_ref[n], table_ref[...], preferred_element_type=F32)
    factor = 1.0 / float(parts * BLK) ** 0.5
    for r in range(rows // 16):
        at = pl.ds(r * 16, 16)
        values = [mixed_ref[n, at, :] for n in range(parts)]
        apart = 1
        while apart < parts:
            values = [
                values[n ^ apart] - values[n] if n & apart else values[n] + values[n ^ apart]
                for n in range(parts)
            ]
            apart *= 2
        for n in range(parts):
            done = values[n] * factor
            if limit is not None:
                done = jnp.clip(done, -limit, limit)
            out_ref[n, at, :] = done.astype(BF)


def both_factors(values, limit=None):
    vmem = pl.BlockSpec(memory_space=pltpu.VMEM)
    return pl.pallas_call(
        functools.partial(hadamard_kernel, limit),
        out_shape=jax.ShapeDtypeStruct(values.shape, BF),
        in_specs=[vmem, vmem],
        out_specs=vmem,
        scratch_shapes=[pltpu.VMEM(values.shape, F32)],
        compiler_params=pltpu.CompilerParams(vmem_limit_bytes=16 * 2**20),
        cost_estimate=pl.CostEstimate(flops=2 * values.size * BLK, bytes_accessed=2_000_000, transcendentals=0),
    )(jnp.asarray(sylvester(BLK), BF), values)


def to_groups(values, parts):
    rows, width = values.shape
    out = values.reshape(2, rows // 2, width // BLK, BLK).transpose(2, 0, 1, 3).reshape(-1, rows // 2, BLK)
    return jnp.pad(out, ((0, parts - out.shape[0]), (0, 0), (0, 0)))


def from_groups(values, width):
    groups = 2 * (width // BLK)
    rows = values.shape[1]
    out = values[:groups].reshape(width // BLK, 2, rows, BLK).transpose(1, 2, 0, 3)
    return out.reshape(2 * rows, width)


def dots_kernel(place_ref, groups_ref, grad_ref, scale_ref, sc_ref, *refs):
    ring = refs[:9]
    partial_ref, rot_ref, total_ref, act_ref = refs[9:]
    zh, y = place_ref[0], place_ref[1]
    n_sc = sc_ref.shape[1]
    n_ring = ring[0].shape[1]
    rows, width = act_ref.shape
    each = rows // 2
    used = 2 * (width // BLK)
    for g in range(used):
        act_ref[(g % 2) * each : (g % 2 + 1) * each, (g // 2) * BLK : (g // 2 + 1) * BLK] = groups_ref[g]
    act_sc = act_ref[:, :n_sc]
    act_ring = act_ref[:, n_sc:]
    dims = (((1,), (1,)), ((), ()))
    for k in range(8):
        shift = (0, -1, 1, -2, 2, -3, 3, 4)[k]
        at = lax.rem(y + shift + 8, 8)
        lanes = pl.multiple_of(lax.rem(at, 2) * BLK, BLK)
        for pair in range(2):
            blocks_sc, blocks_ring, grads, dests = [], [], [], []
            for j in range(2):
                slot = 2 * pair + j
                z = lax.rem(zh + (0, 3, 1, 2)[slot], 4)
                blocks_sc.append(sc_ref[z * 8 + at])
                if k < 7:
                    blocks_ring.append(ring[k][slot])
                else:
                    blocks_ring.append(jnp.concatenate([ring[7][slot], ring[8][slot]], 0))
                dest = z * 4 + lax.div(at, 2)
                dests.append(dest)
                grads.append(grad_ref[dest, :, pl.ds(lanes, BLK)])
            w_sc = jnp.concatenate(blocks_sc, 1)
            w_ring = jnp.concatenate(blocks_ring, 1)
            g = jnp.concatenate(grads, 1)
            part = jnp.dot(act_sc, w_sc, preferred_element_type=F32)
            part += jnp.dot(act_ring, w_ring, preferred_element_type=F32)
            for j in range(2):
                partial_ref[dests[j], :, pl.ds(lanes, BLK)] = part[:, j * BLK : (j + 1) * BLK].astype(BF)
            one = lax.dot_general(g, w_sc, dims, preferred_element_type=F32)
            two = lax.dot_general(g, w_ring, dims, preferred_element_type=F32)
            if k == 0 and pair == 0:
                total_ref[:, :n_sc] = one
                total_ref[:, n_sc:] = two
            else:
                total_ref[:, :n_sc] += one
                total_ref[:, n_sc:] += two
    for g in range(rot_ref.shape[0]):
        if g < used:
            at = slice((g % 2) * each, (g % 2 + 1) * each)
            rot_ref[g] = (total_ref[at, (g // 2) * BLK : (g // 2 + 1) * BLK] * scale_ref[at, :]).astype(BF)
        else:
            rot_ref[g] = jnp.zeros((each, BLK), BF)


def local(hidden, down_rotated, out_gradient, sign_bits, act_exponent, grad_exponent):
    rows, width = hidden.shape
    parts = 16
    cols = out_gradient.shape[1]
    flips = (1 - 2 * sign_bits).astype(F32)
    act_factor = jnp.exp2(act_exponent.astype(F32))[:, None]
    grad_factor = jnp.exp2(grad_exponent.astype(F32))[:, None]

    by_sc = lax.all_gather(down_rotated[:SC_ROWS], DP, axis=0)
    mine = down_rotated[SC_ROWS:]
    own = jnp.stack([mine, shifted(mine, "zh", 1), shifted(mine, "zh", -1), shifted(mine, "zh", 2)])

    signed = (hidden.astype(F32) * flips[None, :] / act_factor).astype(BF)
    act = exchange(both_factors(exchange(to_groups(signed, parts)), 127.0))

    up = down = own
    ring = [own]
    for _ in range(3):
        up, down = shifted(up, "y", 1), shifted(down, "y", -1)
        ring += [up, down]
    half = mine.shape[0] // 2
    ring += [shifted(up[:, :half], "y", 1), shifted(down[:, half:], "y", -1)]

    grad_local = jnp.clip(out_gradient.astype(F32) / grad_factor, -127.0, 127.0).astype(BF)
    grads = exchange(jnp.broadcast_to(grad_local[None], (parts, rows, cols)))

    place = jnp.stack([lax.axis_index("zh"), lax.axis_index("y")]).astype(jnp.int32)
    vmem = pl.BlockSpec(memory_space=pltpu.VMEM)
    partial, rot = pl.pallas_call(
        dots_kernel,
        out_shape=(
            jax.ShapeDtypeStruct((parts, rows, cols), BF),
            jax.ShapeDtypeStruct((parts, rows // 2, BLK), BF),
        ),
        in_specs=[pl.BlockSpec(memory_space=pltpu.SMEM)] + [vmem] * 13,
        out_specs=(vmem, vmem),
        scratch_shapes=[pltpu.VMEM((rows, width), F32), pltpu.VMEM((rows, width), BF)],
        compiler_params=pltpu.CompilerParams(vmem_limit_bytes=40 * 2**20),
        cost_estimate=pl.CostEstimate(flops=4 * rows * width * 4096, bytes_accessed=12_000_000, transcendentals=0),
    )(place, act, grads, grad_factor, by_sc, *ring)

    summed = jnp.sum(exchange(partial).astype(F32), 0)
    mixed = (summed * act_factor).astype(BF)

    back = exchange(both_factors(exchange(rot)))
    grad_hidden = from_groups(back, width).astype(F32) * flips[None, :]
    return mixed, grad_hidden.astype(BF)


def solution(mesh):
    fine = Mesh(mesh.devices.reshape(4, 8, 4, 2, 2), DP + TENSOR)
    in_specs = (P(DP, TENSOR), P(TENSOR, DP), P(DP, TENSOR), P(TENSOR), P(DP), P(DP))
    out_specs = (P(DP, TENSOR), P(DP, TENSOR))
    return jax.shard_map(local, mesh=fine, in_specs=in_specs, out_specs=out_specs, check_vma=False)
```

```python
import functools

import jax
import jax.numpy as jnp
import numpy as np
from jax import lax
from jax.experimental import pallas as pl
from jax.experimental.pallas import tpu as pltpu
from jax.sharding import Mesh, PartitionSpec as P

BLK = 128
TENSOR = ("x", "zl", "core")
DP = ("zh", "y")
BF = jnp.bfloat16
F32 = jnp.float32
SC_ROWS = 448


def sylvester(order):
    index = np.arange(order)
    bits = index[:, None] & index[None, :]
    parity = np.zeros((order, order), np.int64)
    for bit in range(order.bit_length() - 1):
        parity ^= (bits >> bit) & 1
    return 1.0 - 2.0 * parity


def shifted(value, axis, step):
    size = lax.axis_size(axis)
    return lax.ppermute(value, axis, [(i, (i + step) % size) for i in range(size)])


def exchange(value):
    return lax.all_to_all(value, TENSOR, 0, 0)


def hadamard_kernel(limit, table_ref, x_ref, out_ref, mixed_ref):
    parts, rows, _ = x_ref.shape
    for n in range(parts):
        mixed_ref[n] = jnp.dot(x_ref[n], table_ref[...], preferred_element_type=F32)
    factor = 1.0 / float(parts * BLK) ** 0.5
    for r in range(rows // 16):
        at = pl.ds(r * 16, 16)
        values = [mixed_ref[n, at, :] for n in range(parts)]
        apart = 1
        while apart < parts:
            values = [
                values[n ^ apart] - values[n] if n & apart else values[n] + values[n ^ apart]
                for n in range(parts)
            ]
            apart *= 2
        for n in range(parts):
            done = values[n] * factor
            if limit is not None:
                done = jnp.clip(done, -limit, limit)
            out_ref[n, at, :] = done.astype(BF)


def both_factors(values, limit=None):
    vmem = pl.BlockSpec(memory_space=pltpu.VMEM)
    return pl.pallas_call(
        functools.partial(hadamard_kernel, limit),
        out_shape=jax.ShapeDtypeStruct(values.shape, BF),
        in_specs=[vmem, vmem],
        out_specs=vmem,
        scratch_shapes=[pltpu.VMEM(values.shape, F32)],
        compiler_params=pltpu.CompilerParams(vmem_limit_bytes=16 * 2**20),
        cost_estimate=pl.CostEstimate(flops=2 * values.size * BLK, bytes_accessed=2_000_000, transcendentals=0),
    )(jnp.asarray(sylvester(BLK), BF), values)


def to_groups(values, parts):
    rows, width = values.shape
    out = values.reshape(2, rows // 2, width // BLK, BLK).transpose(2, 0, 1, 3).reshape(-1, rows // 2, BLK)
    return jnp.pad(out, ((0, parts - out.shape[0]), (0, 0), (0, 0)))


def from_groups(values, width):
    groups = 2 * (width // BLK)
    rows = values.shape[1]
    out = values[:groups].reshape(width // BLK, 2, rows, BLK).transpose(1, 2, 0, 3)
    return out.reshape(2 * rows, width)


def dots_kernel(place_ref, groups_ref, grad_ref, scale_ref, sc_ref, *refs):
    ring = refs[:9]
    sent_ref, total_ref, act_ref = refs[9:]
    zh, y = place_ref[0], place_ref[1]
    n_sc = sc_ref.shape[1]
    n_ring = ring[0].shape[1]
    rows, width = act_ref.shape
    each = rows // 2
    used = 2 * (width // BLK)
    for g in range(used):
        act_ref[(g % 2) * each : (g % 2 + 1) * each, (g // 2) * BLK : (g // 2 + 1) * BLK] = groups_ref[g]
    act_sc = act_ref[:, :n_sc]
    act_ring = act_ref[:, n_sc:]
    dims = (((1,), (1,)), ((), ()))
    for k in range(8):
        shift = (0, -1, 1, -2, 2, -3, 3, 4)[k]
        at = lax.rem(y + shift + 8, 8)
        lanes = pl.multiple_of(lax.rem(at, 2) * BLK, BLK)
        lines = pl.multiple_of(lax.rem(at, 2) * rows, rows)
        for pair in range(2):
            blocks_sc, blocks_ring, grads, dests = [], [], [], []
            for j in range(2):
                slot = 2 * pair + j
                z = lax.rem(zh + (0, 3, 1, 2)[slot], 4)
                blocks_sc.append(sc_ref[z * 8 + at])
                if k < 7:
                    blocks_ring.append(ring[k][slot])
                else:
                    blocks_ring.append(jnp.concatenate([ring[7][slot], ring[8][slot]], 0))
                dest = z * 4 + lax.div(at, 2)
                dests.append(dest)
                grads.append(grad_ref[dest, :, pl.ds(lanes, BLK)])
            w_sc = jnp.concatenate(blocks_sc, 1)
            w_ring = jnp.concatenate(blocks_ring, 1)
            g = jnp.concatenate(grads, 1)
            part = jnp.dot(act_sc, w_sc, preferred_element_type=F32)
            part += jnp.dot(act_ring, w_ring, preferred_element_type=F32)
            for j in range(2):
                sent_ref[dests[j], pl.ds(lines, rows), :] = part[:, j * BLK : (j + 1) * BLK].astype(BF)
            one = lax.dot_general(g, w_sc, dims, preferred_element_type=F32)
            two = lax.dot_general(g, w_ring, dims, preferred_element_type=F32)
            if k == 0 and pair == 0:
                total_ref[:, :n_sc] = one
                total_ref[:, n_sc:] = two
            else:
                total_ref[:, :n_sc] += one
                total_ref[:, n_sc:] += two
    for g in range(sent_ref.shape[0]):
        if g < used:
            at = slice((g % 2) * each, (g % 2 + 1) * each)
            sent_ref[g, 2 * rows :, :] = (total_ref[at, (g // 2) * BLK : (g // 2 + 1) * BLK] * scale_ref[at, :]).astype(BF)
        else:
            sent_ref[g, 2 * rows :, :] = jnp.zeros((each, BLK), BF)


def local(hidden, down_rotated, out_gradient, sign_bits, act_exponent, grad_exponent):
    rows, width = hidden.shape
    parts = 16
    cols = out_gradient.shape[1]
    flips = (1 - 2 * sign_bits).astype(F32)
    act_factor = jnp.exp2(act_exponent.astype(F32))[:, None]
    grad_factor = jnp.exp2(grad_exponent.astype(F32))[:, None]

    by_sc = lax.all_gather(down_rotated[:SC_ROWS], DP, axis=0)
    mine = down_rotated[SC_ROWS:]
    own = jnp.stack([mine, shifted(mine, "zh", 1), shifted(mine, "zh", -1), shifted(mine, "zh", 2)])

    signed = to_groups((hidden.astype(F32) * flips[None, :] / act_factor).astype(BF), parts)
    grad_local = jnp.clip(out_gradient.astype(F32) / grad_factor, -127.0, 127.0).astype(BF)
    grad_copies = jnp.broadcast_to(grad_local[None], (parts, rows, cols))

    own, signed = lax.optimization_barrier((own, signed))
    up, down = shifted(own, "y", 1), shifted(own, "y", -1)
    ring = [own, up, down]
    grid = both_factors(exchange(signed), 127.0)
    up, down, grid = lax.optimization_barrier((up, down, grid))
    up, down = shifted(up, "y", 1), shifted(down, "y", -1)
    ring += [up, down]
    act = exchange(grid)
    up, down, grad_copies = lax.optimization_barrier((up, down, grad_copies))
    up, down = shifted(up, "y", 1), shifted(down, "y", -1)
    ring += [up, down]
    grads = exchange(grad_copies)
    half = mine.shape[0] // 2
    ring += [shifted(up[:, :half], "y", 1), shifted(down[:, half:], "y", -1)]

    place = jnp.stack([lax.axis_index("zh"), lax.axis_index("y")]).astype(jnp.int32)
    vmem = pl.BlockSpec(memory_space=pltpu.VMEM)
    sent = pl.pallas_call(
        dots_kernel,
        out_shape=jax.ShapeDtypeStruct((parts, 2 * rows + rows // 2, BLK), BF),
        in_specs=[pl.BlockSpec(memory_space=pltpu.SMEM)] + [vmem] * 13,
        out_specs=vmem,
        scratch_shapes=[pltpu.VMEM((rows, width), F32), pltpu.VMEM((rows, width), BF)],
        compiler_params=pltpu.CompilerParams(vmem_limit_bytes=40 * 2**20),
        cost_estimate=pl.CostEstimate(flops=4 * rows * width * 4096, bytes_accessed=12_000_000, transcendentals=0),
    )(place, act, grads, grad_factor, by_sc, *ring)

    arrived = exchange(sent)
    back = exchange(both_factors(arrived[:, 2 * rows :]))
    summed = jnp.sum(arrived[:, : 2 * rows].astype(F32), 0)
    summed = jnp.concatenate([summed[:rows], summed[rows:]], 1)
    mixed = (summed * act_factor).astype(BF)

    grad_hidden = from_groups(back, width).astype(F32) * flips[None, :]
    return mixed, grad_hidden.astype(BF)


def solution(mesh):
    fine = Mesh(mesh.devices.reshape(4, 8, 4, 2, 2), DP + TENSOR)
    in_specs = (P(DP, TENSOR), P(TENSOR, DP), P(DP, TENSOR), P(TENSOR), P(DP), P(DP))
    out_specs = (P(DP, TENSOR), P(DP, TENSOR))
    return jax.shard_map(local, mesh=fine, in_specs=in_specs, out_specs=out_specs, check_vma=False)
```

```python
import functools

import jax
import jax.numpy as jnp
import numpy as np
from jax import lax
from jax.experimental import pallas as pl
from jax.experimental.pallas import tpu as pltpu
from jax.sharding import Mesh, PartitionSpec as P

BLK = 128
TENSOR = ("x", "zl", "core")
DP = ("zh", "y")
BF = jnp.bfloat16
F32 = jnp.float32


def sylvester(order):
    index = np.arange(order)
    bits = index[:, None] & index[None, :]
    parity = np.zeros((order, order), np.int64)
    for bit in range(order.bit_length() - 1):
        parity ^= (bits >> bit) & 1
    return 1.0 - 2.0 * parity


def shifted(value, axis, step):
    size = lax.axis_size(axis)
    return lax.ppermute(value, axis, [(i, (i + step) % size) for i in range(size)])


def turned(value):
    return lax.ppermute(value, ("zh", "x"), [(a * 4 + b, b * 4 + a) for a in range(4) for b in range(4)])


def exchange(value, axes=TENSOR):
    return lax.all_to_all(value, axes, 0, 0)


def to_other_core(value):
    return lax.ppermute(value, "core", [(0, 1), (1, 0)])


def two_to(exponents):
    up = jnp.left_shift(1, jnp.maximum(exponents, 0)).astype(F32)
    down = jnp.left_shift(1, jnp.maximum(exponents, -7) + 7).astype(F32) * (1.0 / 128.0)
    return jnp.where(exponents > 0, up, down)


def groups_of(width, rows):
    half = rows // 2
    for g in range(2 * (width // BLK)):
        yield g, slice((g % 2) * half, (g % 2 + 1) * half), slice((g // 2) * BLK, (g // 2 + 1) * BLK)


def call(kernel, out, arguments, flops, scratch=(), limit=12):
    vmem = pl.BlockSpec(memory_space=pltpu.VMEM)
    smem = pl.BlockSpec(memory_space=pltpu.SMEM)
    return pl.pallas_call(
        kernel,
        out_shape=out,
        in_specs=[smem if a.ndim == 1 else vmem for a in arguments],
        out_specs=jax.tree.map(lambda _: vmem, out),
        scratch_shapes=list(scratch),
        compiler_params=pltpu.CompilerParams(vmem_limit_bytes=limit * 2**20),
        cost_estimate=pl.CostEstimate(flops=flops, bytes_accessed=2_000_000, transcendentals=0),
    )(*arguments)


def spread_kernel(hidden_ref, weight_ref, sign_ref, exponent_ref, out_ref):
    rows, width = hidden_ref.shape
    flips = (1 - 2 * sign_ref[...]).astype(F32)
    scale = two_to(-exponent_ref[...])
    for g, at, units in groups_of(width, rows):
        signed = hidden_ref[at, units].astype(F32) * flips[:, units] * scale[at, :]
        out_ref[g, : rows // 2, :] = signed.astype(BF)
    for b in range(width // BLK):
        block = jnp.transpose(weight_ref[b * BLK : (b + 1) * BLK, :].astype(F32)).astype(BF)
        for h in range(2):
            out_ref[2 * b + h, rows // 2 :, :] = block[h * (BLK // 2) : (h + 1) * (BLK // 2), :]
    for g in range(2 * (width // BLK), out_ref.shape[0]):
        out_ref[g] = jnp.zeros(out_ref.shape[1:], BF)


def hadamard_kernel(clipped, limit, table_ref, x_ref, out_ref, mixed_ref):
    parts, rows, _ = x_ref.shape
    for n in range(parts):
        mixed_ref[n] = jnp.dot(x_ref[n], table_ref[...], preferred_element_type=F32)
    factor = 1.0 / float(parts * BLK) ** 0.5
    for r in range(rows // 16):
        at = pl.ds(r * 16, 16)
        values = [mixed_ref[n, at, :] for n in range(parts)]
        apart = 1
        while apart < parts:
            values = [
                values[n ^ apart] - values[n] if n & apart else values[n] + values[n ^ apart]
                for n in range(parts)
            ]
            apart *= 2
        for n in range(parts):
            done = values[n] * factor
            if r * 16 < clipped:
                done = jnp.clip(done, -limit, limit)
            out_ref[n, at, :] = done.astype(BF)


def forward_kernel(place_ref, weight_ref, own_ref, prev_ref, next_ref, first_ref, second_ref, keep_ref, give_ref, act_ref):
    _, rows, width = act_ref.shape
    split = first_ref.shape[0]
    for g, at, units in groups_of(width, rows):
        act_ref[0, at, units] = own_ref[g]
        act_ref[1, at, units] = prev_ref[g]
        act_ref[2, at, units] = next_ref[g]
        act_ref[3, at, units] = first_ref[g] if g < split else second_ref[g - split]
    core = place_ref[1]
    for out_ref, column in ((give_ref, 1 - core), (keep_ref, core)):
        for zl in range(2):
            at = 2 * (2 * zl + column)
            w = jnp.concatenate([weight_ref[at], weight_ref[at + 1]], 1)
            for k, away in enumerate((0, 3, 1, 2)):
                block = lax.rem(place_ref[0] + away, 4)
                part = jnp.dot(act_ref[k], w, preferred_element_type=F32)
                out_ref[block * 2 + zl] = part.astype(BF)


def back_kernel(place_ref, grad_ref, cross_ref, groups_ref, far_ref, next_ref, prev_ref, kept_ref, weight_ref):
    each, width = groups_ref.shape[2], weight_ref.shape[1]
    for y in range(groups_ref.shape[0]):
        for g in range(groups_ref.shape[1]):
            top = (2 * y + g % 2) * each
            weight_ref[top : top + each, (g // 2) * BLK : (g // 2 + 1) * BLK] = groups_ref[y, g]
    cols = grad_ref.shape[2]
    for out_ref, away in ((far_ref, 2), (next_ref, 1), (prev_ref, 3), (kept_ref, 0)):
        block = lax.rem(place_ref[0] + away, 4)
        total = None
        for from_ref, column in ((grad_ref, place_ref[1]), (cross_ref, 1 - place_ref[1])):
            for zl in range(2):
                w = weight_ref[pl.ds(pl.multiple_of((2 * zl + column) * cols, cols), cols), :]
                term = jnp.dot(from_ref[block * 2 + zl], w, preferred_element_type=F32)
                total = term if total is None else total + term
        out_ref[...] = total.astype(out_ref.dtype)


def local(hidden, down_rotated, out_gradient, sign_bits, act_exponent, grad_exponent):
    rows, width = hidden.shape
    parts = 16
    cols = out_gradient.shape[1]
    half = rows // 2
    used = 2 * (width // BLK)
    lines = half + BLK // 2

    weight = lax.all_gather(down_rotated, "y", axis=0)
    grad_factor = jnp.exp2(grad_exponent.astype(F32))[:, None]
    grad_local = jnp.clip(out_gradient.astype(F32) / grad_factor, -127.0, 127.0).astype(BF)

    spread = jax.ShapeDtypeStruct((parts, lines, BLK), BF)
    signed = call(spread_kernel, spread, (hidden, down_rotated, sign_bits[None, :], act_exponent[:, None]), 1_000_000)
    arrived = exchange(signed)
    arrived, grad_local = lax.optimization_barrier((arrived, grad_local))
    turned_grad = turned(grad_local)
    whole = call(
        functools.partial(hadamard_kernel, half, 127.0),
        spread,
        (jnp.asarray(sylvester(BLK), BF), arrived),
        2 * arrived.size * BLK,
        [pltpu.VMEM((parts, lines, BLK), F32)],
    )
    home = exchange(whole)
    rotated_weight = lax.all_gather(home[:used, half:], "y", axis=0)
    own = home[:used, :half]
    own, turned_grad = lax.optimization_barrier((own, turned_grad))
    grads = exchange(jnp.broadcast_to(turned_grad[None], (parts // 2, rows, cols)), ("x", "zl"))
    cross_grads = to_other_core(grads)
    prev, following = shifted(own, "zh", 1), shifted(own, "zh", -1)
    first, second = shifted(prev[: used // 2], "zh", 1), shifted(following[used // 2 :], "zh", -1)

    place = jnp.stack([lax.axis_index("zh"), lax.axis_index("core")]).astype(jnp.int32)
    dots = 2 * rows * width * 4096
    shares = jax.ShapeDtypeStruct((parts // 2, rows, cols), BF)
    keep, give = call(
        forward_kernel,
        (shares, shares),
        (place, weight, own, prev, following, first, second),
        dots,
        [pltpu.VMEM((4, rows, width), BF)],
    )
    both = (keep.astype(F32) + to_other_core(give).astype(F32)).astype(BF)
    sums = exchange(both, ("x", "zl"))
    block = jax.ShapeDtypeStruct((rows, width), BF)
    far, upper, lower, kept = call(
        back_kernel,
        (block, block, block, jax.ShapeDtypeStruct((rows, width), F32)),
        (place, grads, cross_grads, rotated_weight),
        dots,
        [pltpu.VMEM((4 * cols, width), BF)],
    )
    one, two = shifted(far[:half], "zh", 1), shifted(far[half:], "zh", -1)
    upper = jnp.concatenate([(upper[:half].astype(F32) + one.astype(F32)).astype(BF), upper[half:]])
    lower = jnp.concatenate([lower[:half], (lower[half:].astype(F32) + two.astype(F32)).astype(BF)])
    one, two = shifted(upper, "zh", 1), shifted(lower, "zh", -1)
    flips = (1 - 2 * sign_bits).astype(F32)
    grad_hidden = (kept + one.astype(F32) + two.astype(F32)) * grad_factor * flips[None, :]

    summed = turned(jnp.sum(sums.astype(F32), 0).astype(BF))
    mixed = summed.astype(F32) * jnp.exp2(act_exponent.astype(F32))[:, None]
    return mixed.astype(BF), grad_hidden.astype(BF)


def solution(mesh):
    fine = Mesh(mesh.devices.reshape(4, 8, 4, 2, 2), DP + TENSOR)
    in_specs = (P(DP, TENSOR), P(TENSOR, DP), P(DP, TENSOR), P(TENSOR), P(DP), P(DP))
    out_specs = (P(DP, TENSOR), P(DP, TENSOR))
    return jax.shard_map(local, mesh=fine, in_specs=in_specs, out_specs=out_specs, check_vma=False)
```

```python
import functools

import jax
import jax.numpy as jnp
import numpy as np
from jax import lax
from jax.experimental import pallas as pl
from jax.experimental.pallas import tpu as pltpu
from jax.sharding import Mesh, PartitionSpec as P

BLK = 128
TENSOR = ("x", "zl", "core")
DP = ("zh", "y")
BF = jnp.bfloat16
F32 = jnp.float32


def sylvester(order):
    index = np.arange(order)
    bits = index[:, None] & index[None, :]
    parity = np.zeros((order, order), np.int64)
    for bit in range(order.bit_length() - 1):
        parity ^= (bits >> bit) & 1
    return 1.0 - 2.0 * parity


def shifted(value, axis, step):
    size = lax.axis_size(axis)
    return lax.ppermute(value, axis, [(i, (i + step) % size) for i in range(size)])


def turned(value):
    return lax.ppermute(value, ("zh", "x"), [(a * 4 + b, b * 4 + a) for a in range(4) for b in range(4)])


def exchange(value, axes=TENSOR):
    return lax.all_to_all(value, axes, 0, 0)


def to_other_core(value):
    return lax.ppermute(value, "core", [(0, 1), (1, 0)])


def two_to(exponents):
    up = jnp.left_shift(1, jnp.maximum(exponents, 0)).astype(F32)
    down = jnp.left_shift(1, jnp.maximum(exponents, -7) + 7).astype(F32) * (1.0 / 128.0)
    return jnp.where(exponents > 0, up, down)


def groups_of(width, rows):
    half = rows // 2
    for g in range(2 * (width // BLK)):
        yield g, slice((g % 2) * half, (g % 2 + 1) * half), slice((g // 2) * BLK, (g // 2 + 1) * BLK)


def call(kernel, out, arguments, flops, scratch=(), limit=12):
    vmem = pl.BlockSpec(memory_space=pltpu.VMEM)
    smem = pl.BlockSpec(memory_space=pltpu.SMEM)
    return pl.pallas_call(
        kernel,
        out_shape=out,
        in_specs=[smem if a.ndim == 1 else vmem for a in arguments],
        out_specs=jax.tree.map(lambda _: vmem, out),
        scratch_shapes=list(scratch),
        compiler_params=pltpu.CompilerParams(vmem_limit_bytes=limit * 2**20),
        cost_estimate=pl.CostEstimate(flops=flops, bytes_accessed=2_000_000, transcendentals=0),
    )(*arguments)


def spread_kernel(hidden_ref, weight_ref, sign_ref, exponent_ref, out_ref):
    rows, width = hidden_ref.shape
    flips = (1 - 2 * sign_ref[...]).astype(F32)
    scale = two_to(-exponent_ref[...])
    for g, at, units in groups_of(width, rows):
        signed = hidden_ref[at, units].astype(F32) * flips[:, units] * scale[at, :]
        out_ref[g, : rows // 2, :] = signed.astype(BF)
    for b in range(width // BLK):
        block = jnp.transpose(weight_ref[b * BLK : (b + 1) * BLK, :].astype(F32)).astype(BF)
        for h in range(2):
            out_ref[2 * b + h, rows // 2 :, :] = block[h * (BLK // 2) : (h + 1) * (BLK // 2), :]
    for g in range(2 * (width // BLK), out_ref.shape[0]):
        out_ref[g] = jnp.zeros(out_ref.shape[1:], BF)


def hadamard_kernel(clipped, limit, table_ref, x_ref, out_ref, mixed_ref):
    parts, rows, _ = x_ref.shape
    for n in range(parts):
        mixed_ref[n] = jnp.dot(x_ref[n], table_ref[...], preferred_element_type=F32)
    factor = 1.0 / float(parts * BLK) ** 0.5
    for r in range(rows // 16):
        at = pl.ds(r * 16, 16)
        values = [mixed_ref[n, at, :] for n in range(parts)]
        apart = 1
        while apart < parts:
            values = [
                values[n ^ apart] - values[n] if n & apart else values[n] + values[n ^ apart]
                for n in range(parts)
            ]
            apart *= 2
        for n in range(parts):
            done = values[n] * factor
            if r * 16 < clipped:
                done = jnp.clip(done, -limit, limit)
            out_ref[n, at, :] = done.astype(BF)


def forward_kernel(place_ref, weight_ref, own_ref, prev_ref, next_ref, first_ref, second_ref, keep_ref, give_ref, act_ref):
    _, rows, width = act_ref.shape
    split = first_ref.shape[0]
    for g, at, units in groups_of(width, rows):
        act_ref[0, at, units] = own_ref[g]
        act_ref[1, at, units] = prev_ref[g]
        act_ref[2, at, units] = next_ref[g]
        act_ref[3, at, units] = first_ref[g] if g < split else second_ref[g - split]
    core = place_ref[1]
    for out_ref, column in ((give_ref, 1 - core), (keep_ref, core)):
        for zl in range(2):
            at = 2 * (2 * zl + column)
            w = jnp.concatenate([weight_ref[at], weight_ref[at + 1]], 1)
            for k, away in enumerate((0, 3, 1, 2)):
                block = lax.rem(place_ref[0] + away, 4)
                part = jnp.dot(act_ref[k], w, preferred_element_type=F32)
                out_ref[block * 2 + zl] = part.astype(BF)


def back_kernel(place_ref, grad_ref, cross_ref, groups_ref, far_ref, next_ref, prev_ref, kept_ref, weight_ref):
    each, width = groups_ref.shape[2], weight_ref.shape[1]
    for y in range(groups_ref.shape[0]):
        for g in range(groups_ref.shape[1]):
            top = (2 * y + g % 2) * each
            weight_ref[top : top + each, (g // 2) * BLK : (g // 2 + 1) * BLK] = groups_ref[y, g]
    cols = grad_ref.shape[2]
    for out_ref, away in ((far_ref, 2), (next_ref, 1), (prev_ref, 3), (kept_ref, 0)):
        block = lax.rem(place_ref[0] + away, 4)
        total = None
        for from_ref, column in ((grad_ref, place_ref[1]), (cross_ref, 1 - place_ref[1])):
            for zl in range(2):
                w = weight_ref[pl.ds(pl.multiple_of((2 * zl + column) * cols, cols), cols), :]
                term = jnp.dot(from_ref[block * 2 + zl], w, preferred_element_type=F32)
                total = term if total is None else total + term
        out_ref[...] = total.astype(out_ref.dtype)


def local(hidden, down_rotated, out_gradient, sign_bits, act_exponent, grad_exponent):
    rows, width = hidden.shape
    parts = 16
    cols = out_gradient.shape[1]
    half = rows // 2
    used = 2 * (width // BLK)
    lines = half + BLK // 2

    weight = lax.all_gather(down_rotated, "y", axis=0)
    grad_factor = jnp.exp2(grad_exponent.astype(F32))[:, None]
    grad_local = jnp.clip(out_gradient.astype(F32) / grad_factor, -127.0, 127.0).astype(BF)

    spread = jax.ShapeDtypeStruct((parts, lines, BLK), BF)
    signed = call(spread_kernel, spread, (hidden, down_rotated, sign_bits[None, :], act_exponent[:, None]), 1_000_000)
    arrived = exchange(signed)
    arrived, grad_local = lax.optimization_barrier((arrived, grad_local))
    turned_grad = turned(grad_local)
    whole = call(
        functools.partial(hadamard_kernel, half, 127.0),
        spread,
        (jnp.asarray(sylvester(BLK), BF), arrived),
        2 * arrived.size * BLK,
        [pltpu.VMEM((parts, lines, BLK), F32)],
    )
    home = exchange(whole)
    rotated_weight = lax.all_gather(home[:used, half:], "y", axis=0)
    own = home[:used, :half]
    own, turned_grad = lax.optimization_barrier((own, turned_grad))
    grads = exchange(jnp.broadcast_to(turned_grad[None], (parts // 2, rows, cols)), ("x", "zl"))
    cross_grads = to_other_core(grads)
    prev, following = shifted(own, "zh", 1), shifted(own, "zh", -1)
    first, second = shifted(prev[: used // 2], "zh", 1), shifted(following[used // 2 :], "zh", -1)

    place = jnp.stack([lax.axis_index("zh"), lax.axis_index("core")]).astype(jnp.int32)
    dots = 2 * rows * width * 4096
    shares = jax.ShapeDtypeStruct((parts // 2, rows, cols), BF)
    keep, give = call(
        forward_kernel,
        (shares, shares),
        (place, weight, own, prev, following, first, second),
        dots,
        [pltpu.VMEM((4, rows, width), BF)],
    )
    both = (keep.astype(F32) + to_other_core(give).astype(F32)).astype(BF)
    sums = exchange(both, ("x", "zl"))
    block = jax.ShapeDtypeStruct((rows, width), BF)
    far, upper, lower, kept = call(
        back_kernel,
        (block, block, block, jax.ShapeDtypeStruct((rows, width), F32)),
        (place, grads, cross_grads, rotated_weight),
        dots,
        [pltpu.VMEM((4 * cols, width), BF)],
    )
    one, two = shifted(far[:half], "zh", 1), shifted(far[half:], "zh", -1)
    one, two, sums = lax.optimization_barrier((one, two, sums))
    upper = jnp.concatenate([(upper[:half].astype(F32) + one.astype(F32)).astype(BF), upper[half:]])
    lower = jnp.concatenate([lower[:half], (lower[half:].astype(F32) + two.astype(F32)).astype(BF)])
    one, two = shifted(upper, "zh", 1), shifted(lower, "zh", -1)
    flips = (1 - 2 * sign_bits).astype(F32)
    grad_hidden = (kept + one.astype(F32) + two.astype(F32)) * grad_factor * flips[None, :]

    summed = turned(jnp.sum(sums.astype(F32), 0).astype(BF))
    mixed = summed.astype(F32) * jnp.exp2(act_exponent.astype(F32))[:, None]
    return mixed.astype(BF), grad_hidden.astype(BF)


def solution(mesh):
    fine = Mesh(mesh.devices.reshape(4, 8, 4, 2, 2), DP + TENSOR)
    in_specs = (P(DP, TENSOR), P(TENSOR, DP), P(DP, TENSOR), P(TENSOR), P(DP), P(DP))
    out_specs = (P(DP, TENSOR), P(DP, TENSOR))
    return jax.shard_map(local, mesh=fine, in_specs=in_specs, out_specs=out_specs, check_vma=False)
```

```python
import functools

import jax
import jax.numpy as jnp
import numpy as np
from jax import lax
from jax.experimental import pallas as pl
from jax.experimental.pallas import tpu as pltpu
from jax.sharding import Mesh, PartitionSpec as P

BLK = 128
TENSOR = ("x", "zl", "core")
DP = ("zh", "y")
BF = jnp.bfloat16
F32 = jnp.float32


def sylvester(order):
    index = np.arange(order)
    bits = index[:, None] & index[None, :]
    parity = np.zeros((order, order), np.int64)
    for bit in range(order.bit_length() - 1):
        parity ^= (bits >> bit) & 1
    return 1.0 - 2.0 * parity


def shifted(value, axis, step):
    size = lax.axis_size(axis)
    return lax.ppermute(value, axis, [(i, (i + step) % size) for i in range(size)])


def turned(value):
    return lax.ppermute(value, ("zh", "x"), [(a * 4 + b, b * 4 + a) for a in range(4) for b in range(4)])


def exchange(value, axes=TENSOR):
    return lax.all_to_all(value, axes, 0, 0)


def to_other_core(value):
    return lax.ppermute(value, "core", [(0, 1), (1, 0)])


def two_to(exponents):
    up = jnp.left_shift(1, jnp.maximum(exponents, 0)).astype(F32)
    down = jnp.left_shift(1, jnp.maximum(exponents, -7) + 7).astype(F32) * (1.0 / 128.0)
    return jnp.where(exponents > 0, up, down)


def groups_of(width, rows):
    half = rows // 2
    for g in range(2 * (width // BLK)):
        yield g, slice((g % 2) * half, (g % 2 + 1) * half), slice((g // 2) * BLK, (g // 2 + 1) * BLK)


def call(kernel, out, arguments, flops, scratch=(), limit=12):
    vmem = pl.BlockSpec(memory_space=pltpu.VMEM)
    smem = pl.BlockSpec(memory_space=pltpu.SMEM)
    return pl.pallas_call(
        kernel,
        out_shape=out,
        in_specs=[smem if a.ndim == 1 else vmem for a in arguments],
        out_specs=jax.tree.map(lambda _: vmem, out),
        scratch_shapes=list(scratch),
        compiler_params=pltpu.CompilerParams(vmem_limit_bytes=limit * 2**20),
        cost_estimate=pl.CostEstimate(flops=flops, bytes_accessed=2_000_000, transcendentals=0),
    )(*arguments)


def spread_kernel(hidden_ref, weight_ref, sign_ref, exponent_ref, out_ref):
    rows, width = hidden_ref.shape
    flips = (1 - 2 * sign_ref[...]).astype(F32)
    scale = two_to(-exponent_ref[...])
    for g, at, units in groups_of(width, rows):
        signed = hidden_ref[at, units].astype(F32) * flips[:, units] * scale[at, :]
        out_ref[g, : rows // 2, :] = signed.astype(BF)
    for b in range(width // BLK):
        block = jnp.transpose(weight_ref[b * BLK : (b + 1) * BLK, :].astype(F32)).astype(BF)
        for h in range(2):
            out_ref[2 * b + h, rows // 2 :, :] = block[h * (BLK // 2) : (h + 1) * (BLK // 2), :]
    for g in range(2 * (width // BLK), out_ref.shape[0]):
        out_ref[g] = jnp.zeros(out_ref.shape[1:], BF)


def hadamard_kernel(clipped, limit, table_ref, x_ref, out_ref, mixed_ref):
    parts, rows, _ = x_ref.shape
    for n in range(parts):
        mixed_ref[n] = jnp.dot(x_ref[n], table_ref[...], preferred_element_type=F32)
    factor = 1.0 / float(parts * BLK) ** 0.5
    for r in range(rows // 16):
        at = pl.ds(r * 16, 16)
        values = [mixed_ref[n, at, :] for n in range(parts)]
        apart = 1
        while apart < parts:
            values = [
                values[n ^ apart] - values[n] if n & apart else values[n] + values[n ^ apart]
                for n in range(parts)
            ]
            apart *= 2
        for n in range(parts):
            done = values[n] * factor
            if r * 16 < clipped:
                done = jnp.clip(done, -limit, limit)
            out_ref[n, at, :] = done.astype(BF)


def forward_kernel(place_ref, weight_ref, own_ref, prev_ref, next_ref, first_ref, second_ref, keep_ref, give_ref, act_ref):
    _, rows, width = act_ref.shape
    split = first_ref.shape[0]
    for g, at, units in groups_of(width, rows):
        act_ref[0, at, units] = own_ref[g]
        act_ref[1, at, units] = prev_ref[g]
        act_ref[2, at, units] = next_ref[g]
        act_ref[3, at, units] = first_ref[g] if g < split else second_ref[g - split]
    core = place_ref[1]
    for out_ref, column in ((give_ref, 1 - core), (keep_ref, core)):
        for zl in range(2):
            at = 2 * (2 * zl + column)
            w = jnp.concatenate([weight_ref[at], weight_ref[at + 1]], 1)
            for k, away in enumerate((0, 3, 1, 2)):
                block = lax.rem(place_ref[0] + away, 4)
                part = jnp.dot(act_ref[k], w, preferred_element_type=F32)
                out_ref[block * 2 + zl] = part.astype(BF)


def back_kernel(place_ref, grad_ref, cross_ref, groups_ref, far_ref, next_ref, prev_ref, kept_ref, weight_ref):
    each, width = groups_ref.shape[2], weight_ref.shape[1]
    for y in range(groups_ref.shape[0]):
        for g in range(groups_ref.shape[1]):
            top = (2 * y + g % 2) * each
            weight_ref[top : top + each, (g // 2) * BLK : (g // 2 + 1) * BLK] = groups_ref[y, g]
    cols = grad_ref.shape[2]
    for out_ref, away in ((far_ref, 2), (next_ref, 1), (prev_ref, 3), (kept_ref, 0)):
        block = lax.rem(place_ref[0] + away, 4)
        total = None
        for from_ref, column in ((grad_ref, place_ref[1]), (cross_ref, 1 - place_ref[1])):
            for zl in range(2):
                w = weight_ref[pl.ds(pl.multiple_of((2 * zl + column) * cols, cols), cols), :]
                term = jnp.dot(from_ref[block * 2 + zl], w, preferred_element_type=F32)
                total = term if total is None else total + term
        out_ref[...] = total.astype(out_ref.dtype)


def local(hidden, down_rotated, out_gradient, sign_bits, act_exponent, grad_exponent):
    rows, width = hidden.shape
    parts = 16
    cols = out_gradient.shape[1]
    half = rows // 2
    used = 2 * (width // BLK)
    lines = half + BLK // 2

    weight = lax.all_gather(down_rotated, "y", axis=0)
    grad_factor = jnp.exp2(grad_exponent.astype(F32))[:, None]
    grad_local = jnp.clip(out_gradient.astype(F32) / grad_factor, -127.0, 127.0).astype(BF)

    spread = jax.ShapeDtypeStruct((parts, lines, BLK), BF)
    signed = call(spread_kernel, spread, (hidden, down_rotated, sign_bits[None, :], act_exponent[:, None]), 1_000_000)
    arrived = exchange(signed)
    arrived, grad_local = lax.optimization_barrier((arrived, grad_local))
    turned_grad = turned(grad_local)
    whole = call(
        functools.partial(hadamard_kernel, half, 127.0),
        spread,
        (jnp.asarray(sylvester(BLK), BF), arrived),
        2 * arrived.size * BLK,
        [pltpu.VMEM((parts, lines, BLK), F32)],
    )
    home = exchange(whole)
    rotated_weight = lax.all_gather(home[:used, half:], "y", axis=0)
    own = home[:used, :half]
    own, turned_grad = lax.optimization_barrier((own, turned_grad))
    grads = exchange(jnp.broadcast_to(turned_grad[None], (parts // 2, rows, cols)), ("x", "zl"))
    cross_grads = to_other_core(grads)
    prev, following = shifted(own, "zh", 1), shifted(own, "zh", -1)
    first, second = shifted(prev[: used // 2], "zh", 1), shifted(following[used // 2 :], "zh", -1)

    place = jnp.stack([lax.axis_index("zh"), lax.axis_index("core")]).astype(jnp.int32)
    dots = 2 * rows * width * 4096
    shares = jax.ShapeDtypeStruct((parts // 2, rows, cols), BF)
    keep, give = call(
        forward_kernel,
        (shares, shares),
        (place, weight, own, prev, following, first, second),
        dots,
        [pltpu.VMEM((4, rows, width), BF)],
    )
    both = (keep.astype(F32) + to_other_core(give).astype(F32)).astype(BF)
    sums = exchange(both, ("x", "zl"))
    block = jax.ShapeDtypeStruct((rows, width), BF)
    far, upper, lower, kept = call(
        back_kernel,
        (block, block, block, jax.ShapeDtypeStruct((rows, width), F32)),
        (place, grads, cross_grads, rotated_weight),
        dots,
        [pltpu.VMEM((4 * cols, width), BF)],
    )
    one, two = shifted(far[:half], "zh", 1), shifted(far[half:], "zh", -1)
    summed = jnp.sum(sums.astype(F32), 0).astype(BF)
    one, two, summed = lax.optimization_barrier((one, two, summed))
    summed = turned(summed)
    upper = jnp.concatenate([(upper[:half].astype(F32) + one.astype(F32)).astype(BF), upper[half:]])
    lower = jnp.concatenate([lower[:half], (lower[half:].astype(F32) + two.astype(F32)).astype(BF)])
    one, two = shifted(upper, "zh", 1), shifted(lower, "zh", -1)
    flips = (1 - 2 * sign_bits).astype(F32)
    grad_hidden = (kept + one.astype(F32) + two.astype(F32)) * grad_factor * flips[None, :]

    mixed = summed.astype(F32) * jnp.exp2(act_exponent.astype(F32))[:, None]
    return mixed.astype(BF), grad_hidden.astype(BF)


def solution(mesh):
    fine = Mesh(mesh.devices.reshape(4, 8, 4, 2, 2), DP + TENSOR)
    in_specs = (P(DP, TENSOR), P(TENSOR, DP), P(DP, TENSOR), P(TENSOR), P(DP), P(DP))
    out_specs = (P(DP, TENSOR), P(DP, TENSOR))
    return jax.shard_map(local, mesh=fine, in_specs=in_specs, out_specs=out_specs, check_vma=False)
```

```python
import functools

import jax
import jax.numpy as jnp
import numpy as np
from jax import lax
from jax.experimental import pallas as pl
from jax.experimental.pallas import tpu as pltpu
from jax.sharding import Mesh, PartitionSpec as P

BLK = 128
TENSOR = ("x", "zl", "core")
DP = ("zh", "y")
BF = jnp.bfloat16
F32 = jnp.float32


def sylvester(order):
    index = np.arange(order)
    bits = index[:, None] & index[None, :]
    parity = np.zeros((order, order), np.int64)
    for bit in range(order.bit_length() - 1):
        parity ^= (bits >> bit) & 1
    return 1.0 - 2.0 * parity


def shifted(value, axis, step):
    size = lax.axis_size(axis)
    return lax.ppermute(value, axis, [(i, (i + step) % size) for i in range(size)])


def turned(value):
    return lax.ppermute(value, ("zh", "x"), [(a * 4 + b, b * 4 + a) for a in range(4) for b in range(4)])


def exchange(value, axes=TENSOR):
    return lax.all_to_all(value, axes, 0, 0)


def to_other_core(value):
    return lax.ppermute(value, "core", [(0, 1), (1, 0)])


def two_to(exponents):
    up = jnp.left_shift(1, jnp.maximum(exponents, 0)).astype(F32)
    down = jnp.left_shift(1, jnp.maximum(exponents, -7) + 7).astype(F32) * (1.0 / 128.0)
    return jnp.where(exponents > 0, up, down)


def groups_of(width, rows):
    half = rows // 2
    for g in range(2 * (width // BLK)):
        yield g, slice((g % 2) * half, (g % 2 + 1) * half), slice((g // 2) * BLK, (g // 2 + 1) * BLK)


def call(kernel, out, arguments, flops, scratch=(), limit=12):
    vmem = pl.BlockSpec(memory_space=pltpu.VMEM)
    smem = pl.BlockSpec(memory_space=pltpu.SMEM)
    return pl.pallas_call(
        kernel,
        out_shape=out,
        in_specs=[smem if a.shape == (2,) else vmem for a in arguments],
        out_specs=jax.tree.map(lambda _: vmem, out),
        scratch_shapes=list(scratch),
        compiler_params=pltpu.CompilerParams(vmem_limit_bytes=limit * 2**20),
        cost_estimate=pl.CostEstimate(flops=flops, bytes_accessed=2_000_000, transcendentals=0),
    )(*arguments)


def spread_kernel(hidden_ref, weight_ref, sign_ref, exponent_ref, out_ref):
    rows, width = hidden_ref.shape
    flips = (1 - 2 * sign_ref[...]).astype(F32).reshape(1, width)
    line = two_to(-exponent_ref[...]).reshape(1, rows)
    place = [lax.broadcasted_iota(jnp.int32, (rows, rows), d) for d in range(2)]
    scale = jnp.sum(jnp.where(place[0] == place[1], line, 0.0), 1, keepdims=True)
    for g, at, units in groups_of(width, rows):
        signed = hidden_ref[at, units].astype(F32) * flips[:, units] * scale[at, :]
        out_ref[g, : rows // 2, :] = signed.astype(BF)
    for b in range(width // BLK):
        block = jnp.transpose(weight_ref[b * BLK : (b + 1) * BLK, :].astype(F32)).astype(BF)
        for h in range(2):
            out_ref[2 * b + h, rows // 2 :, :] = block[h * (BLK // 2) : (h + 1) * (BLK // 2), :]
    for g in range(2 * (width // BLK), out_ref.shape[0]):
        out_ref[g] = jnp.zeros(out_ref.shape[1:], BF)


def hadamard_kernel(clipped, limit, table_ref, x_ref, out_ref, mixed_ref):
    parts, rows, _ = x_ref.shape
    for n in range(parts):
        mixed_ref[n] = jnp.dot(x_ref[n], table_ref[...], preferred_element_type=F32)
    factor = 1.0 / float(parts * BLK) ** 0.5
    for r in range(rows // 16):
        at = pl.ds(r * 16, 16)
        values = [mixed_ref[n, at, :] for n in range(parts)]
        apart = 1
        while apart < parts:
            values = [
                values[n ^ apart] - values[n] if n & apart else values[n] + values[n ^ apart]
                for n in range(parts)
            ]
            apart *= 2
        for n in range(parts):
            done = values[n] * factor
            if r * 16 < clipped:
                done = jnp.clip(done, -limit, limit)
            out_ref[n, at, :] = done.astype(BF)


def forward_kernel(place_ref, weight_ref, own_ref, prev_ref, next_ref, first_ref, second_ref, keep_ref, give_ref, act_ref):
    _, rows, width = act_ref.shape
    split = first_ref.shape[0]
    for g, at, units in groups_of(width, rows):
        act_ref[0, at, units] = own_ref[g]
        act_ref[1, at, units] = prev_ref[g]
        act_ref[2, at, units] = next_ref[g]
        act_ref[3, at, units] = first_ref[g] if g < split else second_ref[g - split]
    core = place_ref[1]
    for out_ref, column in ((give_ref, 1 - core), (keep_ref, core)):
        for zl in range(2):
            at = 2 * (2 * zl + column)
            w = jnp.concatenate([weight_ref[at], weight_ref[at + 1]], 1)
            for k, away in enumerate((0, 3, 1, 2)):
                block = lax.rem(place_ref[0] + away, 4)
                part = jnp.dot(act_ref[k], w, preferred_element_type=F32)
                out_ref[block * 2 + zl] = part.astype(BF)


def back_kernel(place_ref, grad_ref, cross_ref, groups_ref, far_ref, next_ref, prev_ref, kept_ref, weight_ref):
    each, width = groups_ref.shape[2], weight_ref.shape[1]
    for y in range(groups_ref.shape[0]):
        for g in range(groups_ref.shape[1]):
            top = (2 * y + g % 2) * each
            weight_ref[top : top + each, (g // 2) * BLK : (g // 2 + 1) * BLK] = groups_ref[y, g]
    cols = grad_ref.shape[2]
    for out_ref, away in ((far_ref, 2), (next_ref, 1), (prev_ref, 3), (kept_ref, 0)):
        block = lax.rem(place_ref[0] + away, 4)
        total = None
        for from_ref, column in ((grad_ref, place_ref[1]), (cross_ref, 1 - place_ref[1])):
            for zl in range(2):
                w = weight_ref[pl.ds(pl.multiple_of((2 * zl + column) * cols, cols), cols), :]
                term = jnp.dot(from_ref[block * 2 + zl], w, preferred_element_type=F32)
                total = term if total is None else total + term
        out_ref[...] = total.astype(out_ref.dtype)


def local(hidden, down_rotated, out_gradient, sign_bits, act_exponent, grad_exponent):
    rows, width = hidden.shape
    parts = 16
    cols = out_gradient.shape[1]
    half = rows // 2
    used = 2 * (width // BLK)
    lines = half + BLK // 2

    weight = lax.all_gather(down_rotated, "y", axis=0)
    grad_factor = jnp.exp2(grad_exponent.astype(F32))[:, None]
    grad_local = jnp.clip(out_gradient.astype(F32) / grad_factor, -127.0, 127.0).astype(BF)

    spread = jax.ShapeDtypeStruct((parts, lines, BLK), BF)
    signed = call(spread_kernel, spread, (hidden, down_rotated, sign_bits, act_exponent), 1_000_000)
    arrived = exchange(signed)
    arrived, grad_local = lax.optimization_barrier((arrived, grad_local))
    turned_grad = turned(grad_local)
    whole = call(
        functools.partial(hadamard_kernel, half, 127.0),
        spread,
        (jnp.asarray(sylvester(BLK), BF), arrived),
        2 * arrived.size * BLK,
        [pltpu.VMEM((parts, lines, BLK), F32)],
    )
    home = exchange(whole)
    rotated_weight = lax.all_gather(home[:used, half:], "y", axis=0)
    own = home[:used, :half]
    own, turned_grad = lax.optimization_barrier((own, turned_grad))
    grads = exchange(jnp.broadcast_to(turned_grad[None], (parts // 2, rows, cols)), ("x", "zl"))
    cross_grads = to_other_core(grads)
    prev, following = shifted(own, "zh", 1), shifted(own, "zh", -1)
    first, second = shifted(prev[: used // 2], "zh", 1), shifted(following[used // 2 :], "zh", -1)

    place = jnp.stack([lax.axis_index("zh"), lax.axis_index("core")]).astype(jnp.int32)
    dots = 2 * rows * width * 4096
    shares = jax.ShapeDtypeStruct((parts // 2, rows, cols), BF)
    keep, give = call(
        forward_kernel,
        (shares, shares),
        (place, weight, own, prev, following, first, second),
        dots,
        [pltpu.VMEM((4, rows, width), BF)],
    )
    both = (keep.astype(F32) + to_other_core(give).astype(F32)).astype(BF)
    sums = exchange(both, ("x", "zl"))
    block = jax.ShapeDtypeStruct((rows, width), BF)
    far, upper, lower, kept = call(
        back_kernel,
        (block, block, block, jax.ShapeDtypeStruct((rows, width), F32)),
        (place, grads, cross_grads, rotated_weight),
        dots,
        [pltpu.VMEM((4 * cols, width), BF)],
    )
    one, two = shifted(far[:half], "zh", 1), shifted(far[half:], "zh", -1)
    one, two, sums = lax.optimization_barrier((one, two, sums))
    upper = jnp.concatenate([(upper[:half].astype(F32) + one.astype(F32)).astype(BF), upper[half:]])
    lower = jnp.concatenate([lower[:half], (lower[half:].astype(F32) + two.astype(F32)).astype(BF)])
    one, two = shifted(upper, "zh", 1), shifted(lower, "zh", -1)
    flips = (1 - 2 * sign_bits).astype(F32)
    grad_hidden = (kept + one.astype(F32) + two.astype(F32)) * grad_factor * flips[None, :]

    summed = turned(jnp.sum(sums.astype(F32), 0).astype(BF))
    mixed = summed.astype(F32) * jnp.exp2(act_exponent.astype(F32))[:, None]
    return mixed.astype(BF), grad_hidden.astype(BF)


def solution(mesh):
    fine = Mesh(mesh.devices.reshape(4, 8, 4, 2, 2), DP + TENSOR)
    in_specs = (P(DP, TENSOR), P(TENSOR, DP), P(DP, TENSOR), P(TENSOR), P(DP), P(DP))
    out_specs = (P(DP, TENSOR), P(DP, TENSOR))
    return jax.shard_map(local, mesh=fine, in_specs=in_specs, out_specs=out_specs, check_vma=False)
```
